32 devices in a mesh: dp: 8 (over z, core), expert: 4 (over y, x).
Axes of the slice: x: 2, y: 2, z: 4, core: 2. Of those that a mesh axis runs over, the one named last changes fastest.
Arguments:
- tokens: bfloat16 [32, 1024, 768], P(('dp', 'expert')), may hold values from -6 to 6
- seg_ids: int32 [32, 1024], P(('dp', 'expert')), may hold values from 0 to 15, never falling along the last dimension, each value on 1 to 512 neighbouring positions
- routes: int32 [32, 1024, 1], P(('dp', 'expert')), may hold values from 0 to 7
- qkv_weight: bfloat16 [768, 2304], P(('dp', 'expert')), may hold values from -0.21875 to 0.21875
- out_weight: bfloat16 [768, 768], P(('dp', 'expert')), may hold values from -1.25 to 1.25
- bias_table: float32 [32, 12], replicated, may hold values from -4 to 4
- norm1_gain: bfloat16 [768], P(('dp', 'expert')), may hold values from 0.5 to 1.5
- norm2_gain: bfloat16 [768], P(('dp', 'expert')), may hold values from 0.5 to 1.5
- router_weight: bfloat16 [768, 8], P(('dp', 'expert')), may hold values from -0.109375 to 0.109375
- expert_in: bfloat16 [8, 3072, 768], P('expert', 'dp'), may hold values from -0.21875 to 0.21875
- expert_out: bfloat16 [8, 3072, 768], P('expert', 'dp'), may hold values from -6 to 6
- upstream: bfloat16 [32, 1024, 768], P(('dp', 'expert')), may hold values from -6 to 6
Outputs:
- block_out: bfloat16 [32, 1024, 768], P(('dp', 'expert'))
- tokens_grad: float32 [32, 1024, 768], P(('dp', 'expert'))
- qkv_weight_grad: float32 [768, 2304], P(('dp', 'expert'))
- out_weight_grad: float32 [768, 768], P(('dp', 'expert'))
- table_grad: float32 [32, 12], replicated
- norm1_grad: float32 [768], P(('dp', 'expert'))
- norm2_grad: float32 [768], P(('dp', 'expert'))
- router_grad: float32 [768, 8], P(('dp', 'expert'))
- expert_in_grad: float32 [8, 3072, 768], P('expert', 'dp')
- expert_out_grad: float32 [8, 3072, 768], P('expert', 'dp')
The draws below stay inside these ranges and needn't reach their ends.
Inputs may be any that keep to these rules, and one draw needn't show every extreme that they name: `seg_ids`: numbers never fall along a sequence; each run of one number is one document of 1 to 512 tokens, and one document has exactly 512. `routes`: every expert is named by some token.
All inputs are finite; a program needn't handle non-finite values.
Results may differ from the reference program's by a relative error of at most 0.017.
Values may be sent and summed in bfloat16 or wider, within the bound.
No kernel may reach another device: no remote copies, remote signals or barrier semaphores. Data moves between devices by JAX's collectives and lax.ppermute only.
A program may use at most 448 MiB of HBM per device.

```python
import math
import jax
import jax.numpy as jnp
import numpy as np
from jax import lax

D = 768
H = 12
HD = 64
FF = 3072
NB = 32
MAXD = 128
LEN = 1024
EXPERTS = 8
TOK_DEV = 1024
SEQS = 32
TOKENS = 32768
CAP = 128
DEVICES = 32


def block_scale(own_key, extent, pieces, smallest, top_value):
    def one(axis_at, blocks):
        steps = jax.random.uniform(jax.random.fold_in(jax.random.fold_in(own_key, 6), axis_at), (blocks,), jnp.float32, smallest / len(pieces), top_value / len(pieces))
        return jnp.repeat(jnp.exp(steps), extent[axis_at] // blocks).reshape((-1,) + (1,) * (len(extent) - axis_at - 1))

    level = one(*pieces[0])
    for cut in pieces[1:]:
        level = level * one(*cut)
    return level


def picks_of(own_key, rows, amount, top, lift):
    order = jax.random.permutation(jax.random.fold_in(own_key, 1), amount)
    favour = order
    for power in range(3):
        favour = favour * favour // amount
    favour = favour * lift // amount
    lots = jax.random.randint(jax.random.fold_in(own_key, 2), (rows, amount), 0, 4096) + favour
    holders = jax.random.permutation(jax.random.fold_in(own_key, 3), rows)[jnp.arange(amount) % rows]
    lots = jnp.where(jnp.arange(rows)[:, None] == holders[None, :], 1 << 14, lots)
    priority = lots * amount + jnp.arange(amount)
    return lax.top_k(priority.astype(jnp.int32), top)[1].astype(jnp.int32)


def length_profile(amount, total, limit, lean):
    weights = [(1 << 20) // math.isqrt(standing ** lean) + 1 for standing in range(2, amount + 1)]
    surplus, counts = total - limit - (amount - 1), [1] * (amount - 1)
    while surplus > 0:
        free = [i for i in range(amount - 1) if counts[i] < limit]
        whole, budget = sum([weights[i] for i in free]), surplus
        for i in free:
            more = min(limit - counts[i], max(1, budget * weights[i] // whole), surplus)
            counts[i] = counts[i] + more
            surplus = surplus - more
    return np.array([limit] + counts)


def uneven_parts(key, number_of, total, limit, skew):
    if number_of == 2:
        one = jax.random.randint(key, (), max(1, total - limit), min(limit, total - 1) + 1)
        return jnp.stack([one, total - one])
    lengths = jnp.asarray(length_profile(number_of, total, limit, skew), jnp.int32)
    pairs = (number_of - 1) // 2
    source_of, sink = lengths[1:1 + 2 * pairs:2], lengths[2:2 + 2 * pairs:2]
    slack = jnp.minimum(source_of - 1, limit - sink)
    moved = jax.random.randint(jax.random.fold_in(key, 1), (pairs,), 0, 1 << 20) % (slack + 1)
    lengths = lengths.at[1:1 + 2 * pairs:2].set(source_of - moved).at[2:2 + 2 * pairs:2].set(sink + moved)
    return lengths[jax.random.permutation(jax.random.fold_in(key, 2), number_of)]


def bell_draw(rng, dims, deviation, most, shards=(), kind=jnp.bfloat16):
    values = jax.random.normal(rng, dims, jnp.float32) * deviation
    if len(shards) > 0:
        values = block_scale(rng, dims, shards, -0.22, 0.18) * values
    return jnp.clip(values, min=-most, max=most).astype(kind)


def setup_inputs(seed: int = 0) -> dict:
    key_of = jax.random.split(jax.random.key(seed), 13)
    return {
        "tokens": bell_draw(key_of[0], (SEQS, LEN, D), 1.0, 6.0, ((0, 32),)),
        "seg_ids": jax.vmap(lambda own: jnp.searchsorted(jnp.cumsum(uneven_parts(own, max(LEN // 64, 4), LEN, LEN // 2, 2)), jnp.arange(LEN), side="right"))(jax.random.split(key_of[1], SEQS)).reshape((SEQS, LEN)).astype(jnp.int32),
        "routes": picks_of(key_of[2], SEQS * LEN, EXPERTS, 1, 1024).reshape((SEQS, LEN, 1)),
        "qkv_weight": bell_draw(key_of[3], (D, 3 * D), D ** -0.5, 0.21875, ((0, 32),)),
        "out_weight": bell_draw(key_of[4], (D, D), (D // 32) ** -0.5, 1.25, ((0, 32),)),
        "bias_table": bell_draw(key_of[5], (NB, H), 1.0, 4.0, (), jnp.float32),
        "norm1_gain": jnp.clip(1.0 + 0.1 * jax.random.normal(key_of[6], (D,), jnp.float32), 0.5, 1.5).astype(jnp.bfloat16),
        "norm2_gain": jnp.clip(1.0 + 0.1 * jax.random.normal(key_of[7], (D,), jnp.float32), 0.5, 1.5).astype(jnp.bfloat16),
        "router_weight": bell_draw(key_of[8], (D, EXPERTS), (4 * D) ** -0.5, 0.109375, ((0, 32),)),
        "expert_in": bell_draw(key_of[9], (EXPERTS, FF, D), D ** -0.5, 0.21875, ((0, 4), (1, 8))),
        "expert_out": bell_draw(key_of[10], (EXPERTS, FF, D), 1 ** -0.5, 6.0, ((0, 4), (1, 8))),
        "upstream": bell_draw(key_of[11], (SEQS, LEN, D), 1.0, 6.0, ((0, 32),)),
    }


EPS = 1e-06
HIGH = lax.Precision.HIGHEST

@jax.custom_vjp
def low(v):
    return lax.optimization_barrier(v.astype(jnp.bfloat16)).astype(jnp.float32)

@jax.custom_vjp
def low_back(v):
    return v

def low_keep(v):
    return (low(v), None)

def low_pass(kept, grad):
    return (grad,)

def back_keep(v):
    return (v, None)

def back_low(kept, grad):
    return (low(grad),)
low.defvjp(low_keep, low_pass)
low_back.defvjp(back_keep, back_low)

def bucket_of_offset(length, buckets, distance):
    offsets = np.arange(-(length - 1), length)
    half_span = buckets // 2
    exact_span = half_span // 2
    upper_side = (offsets > 0).astype(np.int64) * half_span
    magnitude = np.abs(offsets)
    scaled = np.log(np.maximum(magnitude, 1) / exact_span) / np.log(distance / exact_span) * (half_span - exact_span)
    far_bucket = np.minimum(exact_span + np.floor(scaled + 1e-09).astype(np.int64), half_span - 1)
    return (upper_side + np.where(magnitude < exact_span, magnitude, far_bucket)).astype(np.int32)

def rms_norm(values, gain):
    return values * lax.rsqrt(lax.optimization_barrier(jnp.mean(values * values, axis=-1, keepdims=True)) + EPS) * gain

def attend_sequence(inputs, qkv_weight, out_weight, bias_full, gain_one):
    resident, seg_seq = inputs
    normed = low(rms_norm(resident, gain_one))
    qkv_rows = low(low_back(jnp.dot(normed, qkv_weight, precision=HIGH)))
    parts = qkv_rows.reshape(LEN, 3, H, HD)
    queries = parts[:, 0] * HD ** (-0.5)
    scores = jnp.einsum('qhd,khd->hqk', queries, parts[:, 1], precision=HIGH) + bias_full
    same_doc = seg_seq[:, None] == seg_seq[None, :]
    scores = low_back(jnp.where(same_doc[None], scores, -1000000000.0))
    weights = low(jax.nn.softmax(scores, axis=-1))
    attended = jnp.einsum('hqk,khd->qhd', weights, parts[:, 2], precision=HIGH).reshape(LEN, D)
    attended = low(low_back(attended))
    return resident + low_back(jnp.dot(attended, out_weight, precision=HIGH))

def forward(tokens, qkv_weight, out_weight, bias_table, gain_one, gain_two, router_weight, expert_in, expert_out, seg_ids, hot_float, slot_token):
    bucket_ids = jnp.asarray(bucket_of_offset(LEN, NB, MAXD))
    bias_vec = jnp.take(bias_table, bucket_ids, axis=0).T
    positions = jnp.arange(LEN, dtype=jnp.int32)
    offset_grid = positions[None, :] - positions[:, None] + (LEN - 1)
    bias_full = bias_vec[:, offset_grid]

    def attend_one(inputs):
        return attend_sequence(inputs, qkv_weight, out_weight, bias_full, gain_one)
    after_attn = lax.map(jax.checkpoint(attend_one), (tokens, seg_ids)).reshape(TOKENS, D)
    normed = low(rms_norm(after_attn, gain_two))
    logits = low_back(jnp.dot(normed, router_weight, precision=HIGH))
    gate_value = lax.optimization_barrier(jnp.sum(jax.nn.softmax(logits, axis=-1) * hot_float, axis=-1))
    padded = jnp.concatenate([normed, jnp.zeros((1, D), jnp.float32)], axis=0)

    def expert_rows(inputs):
        slots, weight_in, weight_out = inputs
        rows = low_back(padded[slots])
        pre = low_back(jnp.dot(rows, weight_in.T, precision=HIGH))
        hidden = low(jax.nn.gelu(pre, approximate=True))
        return low(low_back(jnp.dot(hidden, weight_out, precision=HIGH)))
    values = lax.map(jax.checkpoint(expert_rows), (slot_token, expert_in, expert_out))
    combined = jnp.zeros((TOKENS + 1, D), jnp.float32).at[slot_token.reshape(-1)].add(values.reshape(-1, D))[:TOKENS]
    return (after_attn + gate_value[:, None] * combined).reshape(SEQS, LEN, D)

def reference(tokens, seg_ids, routes, qkv_weight, out_weight, bias_table, norm1_gain, norm2_gain, router_weight, expert_in, expert_out, upstream):
    route_ids = routes.reshape(TOKENS).astype(jnp.int32)
    route_hot = (route_ids[:, None] == jnp.arange(EXPERTS, dtype=jnp.int32)[None, :]).astype(jnp.int32)
    running = jnp.cumsum(route_hot.reshape(DEVICES, TOK_DEV, EXPERTS), axis=1).reshape(TOKENS, EXPERTS)
    slot_ids = lax.optimization_barrier(jnp.sum(running * route_hot, axis=-1)) - 1
    device_ids = jnp.arange(TOKENS, dtype=jnp.int32) // TOK_DEV
    empty_slot = EXPERTS * DEVICES * CAP
    destination = jnp.where(slot_ids < CAP, route_ids * (DEVICES * CAP) + device_ids * CAP + slot_ids, empty_slot).astype(jnp.int32)
    slot_token = jnp.full((empty_slot + 1,), TOKENS, jnp.int32).at[destination].set(jnp.arange(TOKENS, dtype=jnp.int32))
    slot_token = slot_token[:empty_slot].reshape(EXPERTS, DEVICES * CAP)
    hot_float = route_hot.astype(jnp.float32)

    def closed(tok, wqkv, wout, table, gone, gtwo, wroute, win, wexp):
        return forward(tok, wqkv, wout, table, gone, gtwo, wroute, win, wexp, seg_ids, hot_float, slot_token)
    result, pull = jax.vjp(closed, tokens.astype(jnp.float32), qkv_weight.astype(jnp.float32), out_weight.astype(jnp.float32), bias_table.astype(jnp.float32), norm1_gain.astype(jnp.float32), norm2_gain.astype(jnp.float32), router_weight.astype(jnp.float32), expert_in.astype(jnp.float32), expert_out.astype(jnp.float32))
    grads = pull(upstream.astype(jnp.float32))
    return (result.astype(jnp.bfloat16), grads[0], grads[1], grads[2], grads[3], grads[4], grads[5], grads[6], grads[7], grads[8])
```

```python
import functools

import jax
import jax.numpy as jnp
import numpy as np
from jax import lax
from jax.experimental import pallas as pl
from jax.experimental.pallas import tpu as pltpu
from jax.sharding import PartitionSpec as P

D = 768
H = 12
HD = 64
NB = 32
MAXD = 128
LEN = 1024
EPS = 1e-06

GRP = 4
NG = H // GRP
GW = GRP * HD
QB = 256
NQ = LEN // QB
RB = 512
BT = 128
NEG = -1e9
VMEM = 63 * 1024 * 1024

f32 = jnp.float32
bf16 = jnp.bfloat16


def bucket_of_offset(offsets):
    half_span = NB // 2
    exact_span = half_span // 2
    upper_side = (offsets > 0).astype(np.int64) * half_span
    magnitude = np.abs(offsets)
    scaled = (
        np.log(np.maximum(magnitude, 1) / exact_span)
        / np.log(MAXD / exact_span)
        * (half_span - exact_span)
    )
    far_bucket = np.minimum(exact_span + np.floor(scaled + 1e-09).astype(np.int64), half_span - 1)
    return (upper_side + np.where(magnitude < exact_span, magnitude, far_bucket)).astype(np.int32)


def nt(a, b):
    return lax.dot_general(a, b, (((1,), (1,)), ((), ())), preferred_element_type=f32)


def nn(a, b):
    return lax.dot_general(a, b, (((1,), (0,)), ((), ())), preferred_element_type=f32)


def tn(a, b):
    return lax.dot_general(a, b, (((0,), (0,)), ((), ())), preferred_element_type=f32)


def params(steps=1):
    return pltpu.CompilerParams(
        vmem_limit_bytes=VMEM, dimension_semantics=("arbitrary",) * steps
    )


def cost(flops, size):
    return pl.CostEstimate(flops=int(flops), bytes_accessed=int(size), transcendentals=0)


def whole(shape):
    zeros = (0,) * len(shape)
    return pl.BlockSpec(shape, lambda *_: zeros)


def tiles_kernel(vec, out):
    row = vec[0]
    base = jnp.concatenate([row if i == 0 else pltpu.roll(row, i, 1) for i in range(8)], axis=0)
    for g in range(BT // 8):
        rolled = pltpu.roll(base, (512 - (BT - 8 * g)) % 512, 1)
        for d in range(3):
            out[0, d + 1, 8 * g : 8 * g + 8, :] = rolled[:, d * BT : (d + 1) * BT]
    out[0, 0] = jnp.broadcast_to(row[:, 0:1], (BT, BT))
    out[0, 4] = jnp.broadcast_to(row[:, 511:512], (BT, BT))


def bias_tiles(vectors):
    count = vectors.shape[0]
    return pl.pallas_call(
        tiles_kernel,
        grid=(count,),
        in_specs=[pl.BlockSpec((1, 1, 512), lambda i: (i, 0, 0))],
        out_specs=pl.BlockSpec((1, 5, BT, BT), lambda i: (i, 0, 0, 0)),
        out_shape=jax.ShapeDtypeStruct((count, 5, BT, BT), f32),
        compiler_params=params(),
        cost_estimate=cost(10**9, 10**6),
        name="bias_tiles",
    )(vectors.reshape(count, 1, 512))


def tile_window(bias, head, shift, blocks):
    rows = []
    for a in range(2):
        parts = []
        for b in range(blocks):
            at = jnp.clip(shift + (b - a), -2, 2) + 2
            parts.append(bias[head, at])
        rows.append(jnp.concatenate(parts, axis=1))
    return jnp.concatenate(rows, axis=0)


def head_mask(rows, odd):
    lane = lax.broadcasted_iota(jnp.int32, (rows, 2 * HD), 1)
    return (lane >= HD) if odd else (lane < HD)


def only_head(rows_pair, odd):
    return jnp.where(head_mask(rows_pair.shape[0], odd), rows_pair, jnp.zeros_like(rows_pair))


def attend_kernel(
    experts, rng, tok, wq, wk, wv, tail, segr, segc, bias, normed, qo, ko, vo, ao, lse_out, block
):
    @pl.when(pl.program_id(0) == 0)
    def _():
        gain = jnp.transpose(tail[...].astype(f32))[experts : experts + 1, :]
        for r in range(NQ):
            rows = slice(r * QB, (r + 1) * QB)
            x = tok[rows, :].astype(f32)
            inv = lax.rsqrt(jnp.mean(x * x, axis=-1, keepdims=True) + EPS)
            normed[rows, :] = (x * inv * gain).astype(bf16)

    for r in range(NQ):
        rows = slice(r * QB, (r + 1) * QB)
        n = normed[rows, :]
        qo[rows, :] = nn(n, wq[...]).astype(bf16) * bf16(HD**-0.5)
        ko[rows, :] = nn(n, wk[...]).astype(bf16)
        vo[rows, :] = nn(n, wv[...]).astype(bf16)

    def q_block(qb, carry):
        q0 = pl.multiple_of(qb * QB, QB)
        lo = rng[qb]
        count = rng[NQ + qb]
        k0 = pl.multiple_of(lo * BT, BT)
        for blocks in range(QB // BT, LEN // BT + 1):

            @pl.when(count == blocks)
            def _(blocks=blocks):
                width = blocks * BT
                block[:, :width] = jnp.where(
                    segc[pl.ds(q0, QB), :] == segr[:, pl.ds(k0, width)], 0.0, NEG
                )
                lses = jnp.zeros((QB, 128), f32)
                lane = lax.broadcasted_iota(jnp.int32, (QB, 128), 1)
                for pair in range(GRP // 2):
                    ps = slice(pair * 2 * HD, (pair + 1) * 2 * HD)
                    q_pair = qo[pl.ds(q0, QB), ps]
                    k_pair = ko[pl.ds(k0, width), ps]
                    v_pair = vo[pl.ds(k0, width), ps]
                    outs = []
                    for odd in range(2):
                        head = 2 * pair + odd
                        s = nt(only_head(q_pair, odd), k_pair)
                        s = s + tile_window(bias, head, lo - 2 * qb, blocks) + block[:, :width]
                        top = jnp.max(s, axis=-1, keepdims=True)
                        p = jnp.exp(s - top)
                        total = jnp.sum(p, axis=-1, keepdims=True)
                        o = nn(p.astype(bf16), v_pair)
                        outs.append(o * (1.0 / total))
                        lses = jnp.where(lane == head, top + jnp.log(total), lses)
                    ao[pl.ds(q0, QB), ps] = jnp.where(head_mask(QB, 0), outs[0], outs[1]).astype(
                        bf16
                    )
                lse_out[:, pl.ds(q0, QB)] = jnp.transpose(lses)[0:8, :]

        return carry

    lax.fori_loop(0, NQ, q_block, 0)


def attend(experts, rng, tokens, dense, segr, segc, tiles):
    col = lambda j: pl.BlockSpec((D, GW), lambda g, *_: (0, j * NG + g))
    grp = pl.BlockSpec((LEN, GW), lambda g, *_: (0, g))
    act = jax.ShapeDtypeStruct((LEN, D), bf16)
    return pl.pallas_call(
        functools.partial(attend_kernel, experts),
        grid_spec=pltpu.PrefetchScalarGridSpec(
            num_scalar_prefetch=1,
            grid=(NG,),
            in_specs=[
                whole((LEN, D)),
                col(0),
                col(1),
                col(2),
                pl.BlockSpec((D, 128), lambda g, *_: (0, 4 * D // 128)),
                whole((1, LEN)),
                whole((LEN, 1)),
                pl.BlockSpec((GRP, 5, BT, BT), lambda g, *_: (g, 0, 0, 0)),
            ],
            out_specs=[
                whole((LEN, D)),
                grp,
                grp,
                grp,
                grp,
                pl.BlockSpec((8, LEN), lambda g, *_: (g, 0)),
            ],
            scratch_shapes=[pltpu.VMEM((QB, LEN), f32)],
        ),
        out_shape=[act, act, act, act, act, jax.ShapeDtypeStruct((8 * NG, LEN), f32)],
        compiler_params=params(),
        cost_estimate=cost(10**9, 10**6),
        name="attend",
    )(rng, tokens, dense, dense, dense, dense, segr, segc, tiles)


def route_kernel(experts, tok, att, wout, tail, up, route, dest, after, normed, probs, *rest):
    packs, (acc_n, acc_v) = rest[:-2], rest[-2:]
    step = pl.program_id(0)
    gain = jnp.transpose(tail[...].astype(f32))[experts + 1 : experts + 2, :]
    slots = acc_n.shape[0]
    blocks = [slice(i * QB, (i + 1) * QB) for i in range(RB // QB)]
    for at in blocks:
        after[at, :] = tok[at, :].astype(f32) + nn(att[at, :], wout[...])
    sum_n = sum_v = None
    for at in blocks:
        x = after[at, :]
        inv = lax.rsqrt(jnp.mean(x * x, axis=-1, keepdims=True) + EPS)
        n = (x * inv * gain).astype(bf16)
        normed[at, :] = n
        lane = lax.broadcasted_iota(jnp.int32, (QB, 128), 1)
        logits = jnp.where(lane < experts, nn(n, tail[...]), -jnp.inf)
        e = jnp.exp(logits - jnp.max(logits, axis=-1, keepdims=True))
        p = e / jnp.sum(e, axis=-1, keepdims=True)
        probs[at, :] = p
        gate = jnp.sum(jnp.where(lane == route[at, :], p, 0.0), axis=-1, keepdims=True)
        v = (gate * up[at, :].astype(f32)).astype(bf16)
        slot = lax.broadcasted_iota(jnp.int32, (slots, QB), 0)
        hot = (slot == dest[:, at]).astype(f32).astype(bf16)
        part_n = nn(hot, n)
        part_v = nn(hot, v)
        sum_n = part_n if sum_n is None else sum_n + part_n
        sum_v = part_v if sum_v is None else sum_v + part_v

    @pl.when(step == 0)
    def _():
        acc_n[...] = sum_n
        acc_v[...] = sum_v

    @pl.when(step > 0)
    def _():
        acc_n[...] += sum_n
        acc_v[...] += sum_v

    @pl.when(step == pl.num_programs(0) - 1)
    def _():
        cap = slots // len(packs)
        for i, pack in enumerate(packs):
            pack[0] = acc_n[i * cap : (i + 1) * cap, :].astype(bf16)
            pack[1] = acc_v[i * cap : (i + 1) * cap, :].astype(bf16)


def route_tokens(experts, slots, tokens, att, dense, up, routes, dest_row):
    rows = pl.BlockSpec((RB, D), lambda i: (i, 0))
    act = jax.ShapeDtypeStruct((LEN, D), bf16)
    cap = slots // experts
    outs = pl.pallas_call(
        functools.partial(route_kernel, experts),
        grid=(LEN // RB,),
        in_specs=[
            rows,
            rows,
            pl.BlockSpec((D, D), lambda i: (0, 3)),
            pl.BlockSpec((D, 128), lambda i: (0, 4 * D // 128)),
            rows,
            pl.BlockSpec((RB, 1), lambda i: (i, 0)),
            pl.BlockSpec((1, RB), lambda i: (0, i)),
        ],
        out_specs=[rows, rows, pl.BlockSpec((RB, 128), lambda i: (i, 0))]
        + [whole((2, cap, D))] * experts,
        out_shape=[
            jax.ShapeDtypeStruct((LEN, D), f32),
            act,
            jax.ShapeDtypeStruct((LEN, 128), f32),
        ]
        + [jax.ShapeDtypeStruct((2, cap, D), bf16)] * experts,
        scratch_shapes=[pltpu.VMEM((slots, D), f32), pltpu.VMEM((slots, D), f32)],
        compiler_params=params(),
        cost_estimate=cost(10**9, 10**6),
        name="route_tokens",
    )(tokens, att, dense, dense, up, routes, dest_row)
    return outs[0], outs[1], outs[2], outs[3:]


def expert_kernel(
    size, where, own, other, held, own_out, other_out, out,
    weights, grads, hids, pres, yacc, xacc, in_sem, out_sem,
):
    steps, _, chunk, _ = weights.shape
    peers, _, cap, _ = own.shape
    count = steps * chunk // size
    every = held.shape[1] > steps * chunk

    def load(line):
        at = (2 * line + where[1] if every else line) * size
        src = held.at[:, pl.ds(pl.multiple_of(at, size), size), :]
        step, off = line * size // chunk, line * size % chunk
        dst = weights.at[step, :, pl.ds(off, size), :]
        return pltpu.make_async_copy(src, dst, in_sem.at[line])

    def store(step):
        dst = out.at[:, pl.ds(step * chunk, chunk), :]
        return pltpu.make_async_copy(grads.at[step], dst, out_sem.at[step])

    for line in range(count):
        load(line).start()
    xs = [r[k, 0] for r in (own, other) for k in range(peers)]
    dys = [r[k, 1] for r in (own, other) for k in range(peers)]
    lot = max(QB // cap, 1)
    blocks = 2 * peers // lot
    c0 = np.sqrt(2 / np.pi).astype(np.float32)
    for step in range(steps):
        for line in range(step * chunk // size, (step + 1) * chunk // size):
            load(line).wait()
        wi = weights[step, 0]
        wo = weights[step, 1]

        def ahead(r):
            some = slice(r * lot, (r + 1) * lot)
            return (
                nt(jnp.concatenate(xs[some], axis=0), wi),
                nt(jnp.concatenate(dys[some], axis=0), wo),
            )

        following = ahead(0)
        for r in range(blocks):
            pre, hidden_grad = following
            if r + 1 < blocks:
                following = ahead(r + 1)
            at = slice(r * lot * cap, (r + 1) * lot * cap)
            square = pre * pre
            t = jnp.tanh(c0 * (pre + 0.044715 * (square * pre)))
            cdf = 0.5 * (1.0 + t)
            hidden = (pre * cdf).astype(bf16)
            slope = cdf + (0.5 * pre) * (1.0 - t * t) * (c0 * (1.0 + (3 * 0.044715) * square))
            pre_grad = (hidden_grad * slope).astype(bf16)
            hids[at, :] = hidden
            pres[at, :] = pre_grad
            y = nn(hidden, wo)
            dx = nn(pre_grad, wi)
            if step == 0:
                yacc[at, :] = y
                xacc[at, :] = dx
            else:
                yacc[at, :] += y
                xacc[at, :] += dx
        grads[step, 0] = tn(pres[...], jnp.concatenate(xs, axis=0)).astype(bf16)
        grads[step, 1] = tn(hids[...], jnp.concatenate(dys, axis=0)).astype(bf16)
        store(step).start()
    for i, back in enumerate((own_out, other_out)):
        for k in range(peers):
            at = slice((i * peers + k) * cap, (i * peers + k + 1) * cap)
            back[k, 0] = yacc[at, :].astype(bf16)
            back[k, 1] = xacc[at, :].astype(bf16)
    for step in range(steps):
        store(step).wait()


def expert_step(own, other, held, where):
    peers, _, cap, _ = own.shape
    count = lax.axis_size("dp")
    hidden = 4 * D
    size = hidden // count
    chunk = 768
    steps = hidden // 2 // chunk
    shape = (2, hidden // 2, D)
    any_spec = pl.BlockSpec(memory_space=pl.ANY)
    rows = whole(own.shape)
    acc = pltpu.VMEM((2 * peers * cap, D), f32)
    back = jax.ShapeDtypeStruct(own.shape, bf16)
    return pl.pallas_call(
        functools.partial(expert_kernel, size),
        grid_spec=pltpu.PrefetchScalarGridSpec(
            num_scalar_prefetch=1,
            grid=(1,),
            in_specs=[rows, rows, any_spec],
            out_specs=[rows, rows, any_spec],
            scratch_shapes=[
                pltpu.VMEM((steps, 2, chunk, D), bf16),
                pltpu.VMEM((steps, 2, chunk, D), bf16),
                pltpu.VMEM((2 * peers * cap, chunk), bf16),
                pltpu.VMEM((2 * peers * cap, chunk), bf16),
                acc,
                acc,
                pltpu.SemaphoreType.DMA((count // 2,)),
                pltpu.SemaphoreType.DMA((steps,)),
            ],
        ),
        out_shape=[back, back, jax.ShapeDtypeStruct(shape, bf16)],
        compiler_params=params(),
        cost_estimate=cost(10**9, 10**6),
        name="expert_step",
    )(where, own, other, held)


def join_kernel(experts, after, normed, probs, up, route, dest, att, wout, tail, turned, *refs):
    backs, refs = refs[:experts], refs[experts:]
    block_out, residual, attn_grad, kept, sent, racc, gacc, oacc, ev, rg = refs
    step = pl.program_id(0)
    slots = ev.shape[0]

    @pl.when(step == 0)
    def _():
        cap = slots // experts
        for i, back in enumerate(backs):
            ev[i * cap : (i + 1) * cap, :] = back[0]
            rg[i * cap : (i + 1) * cap, :] = back[1]

    gain = jnp.transpose(tail[...].astype(f32))[experts + 1 : experts + 2, :]
    wt = tail[...]
    wt = jnp.where(lax.broadcasted_iota(jnp.int32, wt.shape, 1) < experts, wt, jnp.zeros_like(wt))
    blocks = [slice(i * QB, (i + 1) * QB) for i in range(RB // QB)]

    def unpack(at):
        slot = lax.broadcasted_iota(jnp.int32, (QB, slots), 1)
        hot = (slot == dest[at, :]).astype(f32).astype(bf16)
        return nn(hot, ev[...]), nn(hot, rg[...])

    unpacked = [unpack(at) for at in blocks]
    branches = []
    logit_grads = []
    gain_part = jnp.zeros((1, D), f32)
    for at, (value, row_grad) in zip(blocks, unpacked):
        lane = lax.broadcasted_iota(jnp.int32, (QB, 128), 1)
        p = probs[at, :]
        own = lane == route[at, :]
        gate = jnp.sum(jnp.where(own, p, 0.0), axis=-1, keepdims=True)
        x = after[at, :]
        upward = up[at, :].astype(f32)
        block_out[at, :] = (x + gate * value).astype(bf16)
        gated = gate * jnp.sum(upward * value, axis=-1, keepdims=True)
        logit_grad = (jnp.where(own, 1.0 - p, -p) * gated).astype(bf16)
        dy = row_grad + nt(logit_grad, wt)
        inv = lax.rsqrt(jnp.mean(x * x, axis=-1, keepdims=True) + EPS)
        scaled = dy * gain
        gain_part = gain_part + jnp.sum(dy * x * inv, axis=0, keepdims=True)
        res = (
            upward
            + inv * scaled
            - x * (inv * inv * inv) * jnp.mean(scaled * x, axis=-1, keepdims=True)
        )
        residual[at, :] = res
        branch = res.astype(bf16)
        attn_grad[at, :] = nt(branch, wout[...]).astype(bf16)
        branches.append(branch)
        logit_grads.append(logit_grad)
    out_part = tn(att[...], jnp.concatenate(branches, axis=0))
    router_part = tn(jnp.concatenate(logit_grads, axis=0), normed[...])

    @pl.when(step == 0)
    def _():
        oacc[...] = out_part
        racc[...] = router_part
        gacc[...] = gain_part

    @pl.when(step > 0)
    def _():
        oacc[...] += out_part
        racc[...] += router_part
        gacc[...] += gain_part

    @pl.when(step == pl.num_programs(0) - 1)
    def _():
        sub = lax.broadcasted_iota(jnp.int32, (128, D), 0)
        extra = jnp.where(sub == experts, gacc[...], racc[...]).astype(bf16)
        term = oacc[...].astype(bf16)
        for half, rows in ((kept, slice(0, D // 2)), (sent, slice(D // 2, D))):
            half[:, :D] = nn(turned[rows, :], term).astype(bf16)
            half[:, D:] = nt(turned[rows, :], extra).astype(bf16)


def join(experts, after, normed, probs, up, routes, dest_col, att, dense, turned, backs):
    rows = pl.BlockSpec((RB, D), lambda i: (i, 0))
    thin = pl.BlockSpec((RB, 1), lambda i: (i, 0))
    cap = backs[0].shape[1]
    act = jax.ShapeDtypeStruct((LEN, D), bf16)
    return pl.pallas_call(
        functools.partial(join_kernel, experts),
        grid=(LEN // RB,),
        in_specs=[
            rows,
            rows,
            pl.BlockSpec((RB, 128), lambda i: (i, 0)),
            rows,
            thin,
            thin,
            rows,
            pl.BlockSpec((D, D), lambda i: (0, 3)),
            pl.BlockSpec((D, 128), lambda i: (0, 4 * D // 128)),
            whole((D, D)),
        ]
        + [whole((2, cap, D))] * experts,
        out_specs=[rows, rows, rows, whole((D // 2, D + 128)), whole((D // 2, D + 128))],
        out_shape=[
            act,
            jax.ShapeDtypeStruct((LEN, D), f32),
            act,
            jax.ShapeDtypeStruct((D // 2, D + 128), bf16),
            jax.ShapeDtypeStruct((D // 2, D + 128), bf16),
        ],
        scratch_shapes=[
            pltpu.VMEM((128, D), f32),
            pltpu.VMEM((1, D), f32),
            pltpu.VMEM((D, D), f32),
            pltpu.VMEM((experts * cap, D), bf16),
            pltpu.VMEM((experts * cap, D), bf16),
        ],
        compiler_params=params(),
        cost_estimate=cost(10**9, 10**6),
        name="join",
    )(after, normed, probs, up, routes, dest_col, att, dense, dense, turned, *backs)


def back_kernel(
    experts, final, rng, q, k, v, dout, att, lse, segr, segc, bias, normed, wq, wk, wv, turned, *refs
):
    if final:
        dxn_in, tok, residual, tail, kept, sent, zvec, tokens_grad = refs[:8]
        dxn, normed_t, dq, gk, gv, tiles, block, delta = refs[8:]
    else:
        kept, sent, zvec, dxn, normed_t, dq, gk, gv, tiles, block, delta = refs
    g = pl.program_id(0)

    @pl.when(g == 0)
    def _():
        normed_t[...] = nt(turned[...], normed[...]).astype(bf16)
        dxn[...] = dxn_in[...] if final else jnp.zeros_like(dxn)

    dq[...] = jnp.zeros_like(dq)
    tiles[...] = jnp.zeros_like(tiles)
    sel = (
        lax.broadcasted_iota(jnp.int32, (8, GW), 1) // HD
        == lax.broadcasted_iota(jnp.int32, (8, GW), 0)
    ).astype(f32)
    delta[...] = lax.dot_general(
        sel,
        dout[...].astype(f32) * att[...].astype(f32),
        (((1,), (1,)), ((), ())),
        precision=lax.Precision.HIGHEST,
        preferred_element_type=f32,
    )

    def k_block(kb, carry):
        k0 = pl.multiple_of(kb * QB, QB)
        lo = rng[kb]
        count = rng[NQ + kb]
        q0 = pl.multiple_of(lo * BT, BT)
        for blocks in range(QB // BT, LEN // BT + 1):

            @pl.when(count == blocks)
            def _(blocks=blocks):
                width = blocks * BT
                block[:, :width] = jnp.where(
                    segc[pl.ds(k0, QB), :] == segr[:, pl.ds(q0, width)], 0.0, NEG
                )
                for pair in range(GRP // 2):
                    ps = slice(pair * 2 * HD, (pair + 1) * 2 * HD)
                    k_pair = k[pl.ds(k0, QB), ps]
                    v_pair = v[pl.ds(k0, QB), ps]
                    q_pair = q[pl.ds(q0, width), ps]
                    do_pair = dout[pl.ds(q0, width), ps]
                    dk_sum = None
                    dv_sum = None
                    dq_sum = None
                    for odd in range(2):
                        head = 2 * pair + odd
                        qm = only_head(q_pair, odd)
                        dom = only_head(do_pair, odd)
                        km = only_head(k_pair, odd)
                        s = nt(k_pair, qm)
                        s = s + tile_window(bias, head, lo - 2 * kb, blocks) + block[:, :width]
                        p = jnp.exp(s - lse[head : head + 1, pl.ds(q0, width)])
                        ds = p * (nt(v_pair, dom) - delta[head : head + 1, pl.ds(q0, width)])
                        for a in range(2):
                            for b in range(blocks):
                                at = jnp.clip(lo - 2 * kb + (b - a), -2, 2) + 2
                                tiles[head, at] += ds[
                                    a * BT : (a + 1) * BT, b * BT : (b + 1) * BT
                                ]
                        pb = p.astype(bf16)
                        dsb = ds.astype(bf16)
                        dv_part = nn(pb, dom)
                        dk_part = nn(dsb, qm)
                        dq_part = tn(dsb, km)
                        dv_sum = dv_part if dv_sum is None else dv_sum + dv_part
                        dk_sum = dk_part if dk_sum is None else dk_sum + dk_part
                        dq_sum = dq_part if dq_sum is None else dq_sum + dq_part
                    gk[pl.ds(k0, QB), ps] = dk_sum.astype(bf16)
                    gv[pl.ds(k0, QB), ps] = dv_sum.astype(bf16)
                    dq[pl.ds(q0, width), ps] += dq_sum

        return carry

    lax.fori_loop(0, NQ, k_block, 0)

    gq = (dq[...] * HD**-0.5).astype(bf16)
    for half, rows in ((kept, slice(0, D // 2)), (sent, slice(D // 2, D))):
        half[:, 0:GW] = nn(normed_t[rows, :], gq).astype(bf16)
        half[:, GW : 2 * GW] = nn(normed_t[rows, :], gk[...]).astype(bf16)
        half[:, 2 * GW : 3 * GW] = nn(normed_t[rows, :], gv[...]).astype(bf16)
    dxn[...] += nt(gq, wq[...]) + nt(gk[...], wk[...]) + nt(gv[...], wv[...])

    rows = []
    for head in range(GRP):
        total = jnp.zeros((8, 512), f32)
        for i in range(BT // 8):
            part = [tiles[head, d, 8 * i : 8 * i + 8, :] for d in range(1, 4)]
            part = jnp.concatenate(part + [jnp.zeros((8, BT), f32)], axis=1)
            total = total + pltpu.roll(part, BT - 8 * i, 1)
        row = total[0:1, :]
        for i in range(1, 8):
            row = row + pltpu.roll(total[i : i + 1, :], 512 - i, 1)
        below = jnp.sum(tiles[head, 0], axis=0, keepdims=True)
        above = jnp.sum(tiles[head, 4], axis=0, keepdims=True)
        rows.append(row + jnp.concatenate([below, jnp.zeros((1, 2 * BT), f32), above], axis=1))
    zvec[...] = jnp.concatenate(rows + [jnp.zeros((8 - GRP, 512), f32)], axis=0)

    def finish():
        gain = jnp.transpose(tail[...].astype(f32))[experts : experts + 1, :]
        total = jnp.zeros((1, D), f32)
        for r in range(NQ):
            at = slice(r * QB, (r + 1) * QB)
            x = tok[at, :].astype(f32)
            inv = lax.rsqrt(jnp.mean(x * x, axis=-1, keepdims=True) + EPS)
            dy = dxn[at, :]
            scaled = dy * gain
            total = total + jnp.sum(dy * x * inv, axis=0, keepdims=True)
            tokens_grad[at, :] = (
                residual[at, :]
                + inv * scaled
                - x * (inv * inv * inv) * jnp.mean(scaled * x, axis=-1, keepdims=True)
            )
        total = jnp.broadcast_to(total, (128, D)).astype(bf16)
        for half, rows in ((kept, slice(0, D // 2)), (sent, slice(D // 2, D))):
            half[:, 3 * GW :] = nt(turned[rows, :], total).astype(bf16)

    if final:
        pl.when(g == pl.num_programs(0) - 1)(finish)


def attend_back(experts, rng, start, count, operands, last=None):
    q, k, v, dout, att, lse, segr, segc, tiles, normed, dense, turned = operands
    col = lambda j: pl.BlockSpec((D, GW), lambda g, *_: (0, j * NG + start + g))
    grp = pl.BlockSpec((LEN, GW), lambda g, *_: (0, start + g))
    final = last is not None
    act = jax.ShapeDtypeStruct((LEN, D), f32)
    in_specs = [
        grp,
        grp,
        grp,
        grp,
        grp,
        pl.BlockSpec((8, LEN), lambda g, *_: (start + g, 0)),
        whole((1, LEN)),
        whole((LEN, 1)),
        pl.BlockSpec((GRP, 5, BT, BT), lambda g, *_: (NG + start + g, 0, 0, 0)),
        whole((LEN, D)),
        col(0),
        col(1),
        col(2),
        whole((D, D)),
    ]
    args = [q, k, v, dout, att, lse, segr, segc, tiles, normed, dense, dense, dense, turned]
    wide = 3 * GW + 128 if final else 3 * GW
    out_specs = [
        pl.BlockSpec((D // 2, wide), lambda g, *_: (0, g)),
        pl.BlockSpec((D // 2, wide), lambda g, *_: (0, g)),
        pl.BlockSpec((8, 512), lambda g, *_: (g, 0)),
    ]
    out_shape = [
        jax.ShapeDtypeStruct((D // 2, count * wide), bf16),
        jax.ShapeDtypeStruct((D // 2, count * wide), bf16),
        jax.ShapeDtypeStruct((8 * count, 512), f32),
    ]
    scratch = [
        pltpu.VMEM((D, LEN), bf16),
        pltpu.VMEM((LEN, GW), f32),
        pltpu.VMEM((LEN, GW), bf16),
        pltpu.VMEM((LEN, GW), bf16),
        pltpu.VMEM((GRP, 5, BT, BT), f32),
        pltpu.VMEM((QB, LEN), f32),
        pltpu.VMEM((8, LEN), f32),
    ]
    if final:
        in_specs += [
            whole((LEN, D)),
            whole((LEN, D)),
            whole((LEN, D)),
            pl.BlockSpec((D, 128), lambda g, *_: (0, 4 * D // 128)),
        ]
        args += list(last) + [dense]
        out_specs.append(whole((LEN, D)))
        out_shape.append(act)
        scratch = [pltpu.VMEM((LEN, D), f32)] + scratch
    else:
        out_specs.append(whole((LEN, D)))
        out_shape.append(act)
    outs = pl.pallas_call(
        functools.partial(back_kernel, experts, final),
        grid_spec=pltpu.PrefetchScalarGridSpec(
            num_scalar_prefetch=1,
            grid=(count,),
            in_specs=in_specs,
            out_specs=out_specs,
            scratch_shapes=scratch,
        ),
        out_shape=out_shape,
        compiler_params=params(),
        cost_estimate=cost(10**9, 10**6),
        name="attend_back",
    )(rng, *args)
    return outs


def along_z(rows, k):
    size = lax.axis_size("dp")
    return lax.ppermute(rows, "dp", [(i, (i + 2 * k) % size) for i in range(size)])


def other_core(rows):
    return lax.ppermute(rows, "dp", [(i, i ^ 1) for i in range(lax.axis_size("dp"))])


def peer(rows, k):
    return lax.ppermute(rows, "expert", [(i, i ^ k) for i in range(lax.axis_size("expert"))])


def place_kernel(where, own, swapped, out):
    z, core, me = where[0], where[1], where[2]
    peers, depth = own.shape[:2]
    for k in range(peers):
        for j in range(depth):
            line = 2 * lax.rem(z - j + depth, depth)
            out[(line + core) * peers + (me ^ k)] = own[k, j]
            out[(line + 1 - core) * peers + (me ^ k)] = swapped[k, j]


def gather_dense(block, where, middle):
    peers = lax.axis_size("expert")
    depth = lax.axis_size("dp") // 2
    block = block[None]
    line = [along_z(block, k) for k in range(1, depth)]
    column = jnp.concatenate([block] + line, axis=0)
    plane = jnp.stack([column] + [peer(column, k) for k in range(1, peers)])
    plane, middle = lax.optimization_barrier((plane, middle))
    shape = (2 * peers * depth,) + block.shape[1:]
    out = pl.pallas_call(
        place_kernel,
        grid_spec=pltpu.PrefetchScalarGridSpec(
            num_scalar_prefetch=1,
            grid=(1,),
            in_specs=[whole(plane.shape), whole(plane.shape)],
            out_specs=whole(shape),
        ),
        out_shape=jax.ShapeDtypeStruct(shape, bf16),
        compiler_params=params(),
        cost_estimate=cost(10**9, 10**7),
        name="place_rows",
    )(where, plane, other_core(plane))
    return out.reshape(-1, block.shape[2]), line, middle


def in_parts(numbers, width):
    high = lax.reduce_precision(numbers, 8, 7)
    low = lax.reduce_precision(numbers - high, 8, 7)
    row = jnp.concatenate([high, low, jnp.zeros((width - 2 * numbers.shape[0],), f32)])
    row = jnp.concatenate([row[None], jnp.zeros((15, width), f32)]).astype(bf16)
    return high + low, row


def from_parts(row, count):
    row = row.astype(f32)
    return row[:count] + row[count : 2 * count]


def tree_sum(parts):
    while len(parts) > 1:
        parts = [parts[i] + parts[i + 1] for i in range(0, len(parts), 2)]
    return parts[0]


def stage(total, partners, move, numbers=None):
    size = total.shape[0] // partners
    pieces = [total[k * size : (k + 1) * size] for k in range(partners)]
    if numbers is None:
        moved = [move(pieces[k], k) for k in range(1, partners)]
    else:
        kept, row = in_parts(numbers, total.shape[1])
        moved = [move(jnp.concatenate([pieces[k], row]), k) for k in range(1, partners)]
        count = numbers.shape[0]
        numbers = tree_sum([kept] + [from_parts(m[size], count) for m in moved])
    return sum([m[:size].astype(f32) for m in moved], pieces[0].astype(f32)), numbers


def over_cores(kept, sent, numbers=None):
    total = [k.astype(f32) + other_core(s).astype(f32) for k, s in zip(kept, sent)]
    if numbers is not None:
        mine, row = in_parts(numbers, 2 * numbers.shape[0])
        numbers = mine + from_parts(other_core(row)[0], numbers.shape[0])
    return jnp.concatenate(total, axis=1).astype(bf16), numbers


def to_line(rows, k):
    size = lax.axis_size("dp")
    return lax.ppermute(rows, "dp", [(i, i ^ (2 * k)) for i in range(size)])


def body(
    tokens,
    seg_ids,
    routes,
    qkv_weight,
    out_weight,
    bias_table,
    norm1_gain,
    norm2_gain,
    router_weight,
    expert_in,
    expert_out,
    upstream,
):
    experts = router_weight.shape[1]
    own_rows = qkv_weight.shape[0]
    capacity = LEN // experts
    slots = experts * capacity
    local_experts = expert_in.shape[0]
    peers = experts // local_experts

    index = lax.axis_index("dp")
    own = lax.axis_index("expert")
    depth = lax.axis_size("dp") // 2
    where = jnp.stack([index // 2, index % 2, own]).astype(jnp.int32)

    rows = jnp.arange(D)
    chunk, row = rows // own_rows, rows % own_rows
    c_rel, e_rel, z_rel = chunk // (peers * depth), chunk // depth % peers, chunk % depth
    line_at = (index // 2 ^ z_rel) * 2 + (index % 2 ^ c_rel)
    source = (line_at * peers + (own ^ e_rel)) * own_rows + row
    turned = (source[:, None] == jnp.arange(D)[None, :]).astype(bf16)

    offsets = np.arange(512) - 256
    hot_fwd = (bucket_of_offset(offsets)[None, :] == np.arange(NB)[:, None]).astype(np.float32)
    hot_bwd = (bucket_of_offset(-offsets)[None, :] == np.arange(NB)[:, None]).astype(np.float32)
    table = bias_table.T
    vectors = jnp.concatenate(
        [
            jnp.dot(table, hot_fwd, precision=lax.Precision.HIGHEST),
            jnp.dot(table, hot_bwd, precision=lax.Precision.HIGHEST),
        ],
        axis=0,
    )
    tiles = bias_tiles(vectors)

    seg = seg_ids.reshape(LEN)
    first = seg.reshape(NQ, QB)[:, 0]
    last = seg.reshape(NQ, QB)[:, QB - 1]
    low = jnp.sum((seg[None, :] < first[:, None]).astype(jnp.int32), axis=1) // BT
    high = (jnp.sum((seg[None, :] <= last[:, None]).astype(jnp.int32), axis=1) + BT - 1) // BT
    rng = jnp.concatenate([low, high - low])
    segr = seg.reshape(1, LEN)
    segc = seg.reshape(LEN, 1)

    route_col = routes.reshape(LEN, 1)
    hot = (route_col == jnp.arange(experts, dtype=jnp.int32)[None, :]).astype(jnp.int32)
    slot_ids = jnp.sum(jnp.cumsum(hot, axis=0) * hot, axis=-1) - 1
    owner = (route_col[:, 0] // local_experts) ^ own
    pack_at = (route_col[:, 0] % local_experts) * peers + owner
    dest = jnp.where(slot_ids < capacity, pack_at * capacity + slot_ids, slots)
    dest_row = dest.reshape(1, LEN)
    dest_col = dest.reshape(LEN, 1)

    dense, line, middle = gather_dense(
        jnp.concatenate(
            [
                qkv_weight,
                out_weight,
                router_weight,
                norm1_gain[:, None],
                norm2_gain[:, None],
                jnp.zeros((own_rows, 128 - experts - 2), bf16),
            ],
            axis=1,
        ),
        where,
        (tiles, rng, segc, dest_row, dest_col, turned),
    )
    tiles, rng, segc, dest_row, dest_col, turned = middle
    stacks = [jnp.stack([expert_in[e], expert_out[e]]) for e in range(local_experts)]
    stacks = lax.optimization_barrier(stacks)
    cores = [list(range(c, 2 * depth, 2)) for c in range(2)]
    pieces = [
        lax.all_gather(w, "dp", axis=1, tiled=True, axis_index_groups=None if e else cores)
        for e, w in enumerate(stacks)
    ]

    tok = tokens.reshape(LEN, D)
    up = upstream.reshape(LEN, D)
    normed_one, q, k, v, att, lse = attend(experts, rng, tok, dense, segr, segc, tiles)
    after, normed_two, probs, packs = route_tokens(
        experts, slots, tok, att, dense, up, route_col, dest_row
    )

    def exchange(rows):
        return [rows[0]] + [peer(rows[j], j) for j in range(1, peers)]

    travelling = exchange(packs[:peers])
    sent = None
    backs = []
    shares = []
    for e in range(local_experts):
        if e:
            travelling, sent = lax.optimization_barrier((travelling, sent))
            backs = backs + exchange([sent[j] for j in range(peers)])
        rows = jnp.stack(travelling)
        received = (rows, other_core(rows))
        if e + 1 < local_experts:
            packs, received = lax.optimization_barrier((packs, received))
            travelling = exchange(packs[(e + 1) * peers : (e + 2) * peers])
        own_part, other_part, grads = expert_step(*received, pieces[e], where)
        other_part, own_part, travelling, backs = lax.optimization_barrier(
            (other_part, own_part, travelling, backs)
        )
        sent = (own_part.astype(f32) + other_core(other_part).astype(f32)).astype(bf16)
        if e:
            sent, grads, backs = lax.optimization_barrier((sent, grads, backs))
        shares.append(
            lax.psum_scatter(
                grads, "dp", scatter_dimension=1, tiled=True, axis_index_groups=cores
            )
        )
    backs = backs + exchange([sent[j] for j in range(peers)])

    block_out, residual, attn_grad, out_kept, out_sent = join(
        experts, after, normed_two, probs, up, route_col, dest_col, att, dense, turned, backs
    )
    operands = (q, k, v, attn_grad, att, lse, segr, segc, tiles, normed_one, dense, turned)
    split = NG - 1
    kept_a, sent_a, z_a, dxn = attend_back(experts, rng, 0, split, operands)
    part_a, _ = over_cores([kept_a, out_kept], [sent_a, out_sent])
    part_a, dxn, shares[:-1] = lax.optimization_barrier((part_a, dxn, shares[:-1]))
    part_a, _ = stage(part_a, peers, peer)
    kept_b, sent_b, z_b, tokens_grad = attend_back(
        experts, rng, split, NG - split, operands, (dxn, tok, residual)
    )
    kept_b, sent_b, z_b, part_a, shares = lax.optimization_barrier(
        (kept_b, sent_b, z_b, part_a, shares)
    )
    z = jnp.concatenate([z_a, z_b], axis=0).reshape(NG, 8, 512)[:, :GRP].reshape(H, 512)
    table = lax.dot_general(hot_bwd, z, (((1,), (1,)), ((), ())), precision=lax.Precision.HIGHEST)
    part_b, table = over_cores([kept_b], [sent_b], table.reshape(NB * H))
    part_b, table = stage(part_b, peers, peer, table)
    part = jnp.concatenate([part_a.astype(bf16), part_b.astype(bf16)], axis=1)
    share, table = stage(part, depth, to_line, table)
    table_grad = table.reshape(NB, H)
    wide = split * D + D + 128
    qkv_share = jnp.concatenate([share[:, : split * D], share[:, wide : wide + D]], axis=1)
    qkv_share = (
        qkv_share.reshape(own_rows, NG, 3, GW).transpose(0, 2, 1, 3).reshape(own_rows, 3 * D)
    )
    out_share = share[:, split * D : wide]
    shares = [part.astype(f32) for part in shares]
    return (
        block_out.reshape(tokens.shape),
        tokens_grad.reshape(tokens.shape),
        qkv_share,
        out_share[:, :D],
        table_grad,
        share[:, wide + D],
        out_share[:, D + experts],
        out_share[:, D : D + experts],
        jnp.stack([share[0] for share in shares]),
        jnp.stack([share[1] for share in shares]),
    )


def solution(mesh):
    both = ("dp", "expert")
    in_specs = (
        P(both, None, None),
        P(both, None),
        P(both, None, None),
        P(both, None),
        P(both, None),
        P(),
        P(both),
        P(both),
        P(both, None),
        P("expert", "dp", None),
        P("expert", "dp", None),
        P(both, None, None),
    )
    out_specs = (
        P(both, None, None),
        P(both, None, None),
        P(both, None),
        P(both, None),
        P(),
        P(both),
        P(both),
        P(both, None),
        P("expert", "dp", None),
        P("expert", "dp", None),
    )
    return jax.shard_map(body, mesh=mesh, in_specs=in_specs, out_specs=out_specs, check_vma=False)
```
